32 devices in a mesh: dp: 8 (over y, x, core), seq: 4 (over z).
Axes of the slice: x: 2, y: 2, z: 4, core: 2. Of those that a mesh axis runs over, the one named last changes fastest.
Arguments:
- signal: bfloat16 [8, 2048, 1408], P('dp', 'seq'), may hold values from -240 to 240
- bases: int32 [8, 2048], P('dp', 'seq'), may hold values from 0 to 3
- base_table: bfloat16 [4, 1408], replicated, may hold values from -6 to 6
- conv_weight: bfloat16 [5, 1408, 1408], P(None, None, 'dp'), may hold values from -0.0625 to 0.0625
- batch_norm_gain: float32 [1408], replicated, may hold values from 0.1 to 1.9
- norm_bias: float32 [1408], replicated, may hold values from -3 to 3
- proj_weight: bfloat16 [1408, 1536], replicated, may hold values from -0.15625 to 0.15625
- attn_gain: float32 [1536], replicated, may hold values from 0.1 to 1.9
- q_weight: bfloat16 [1536, 1024], replicated, may hold values from -2 to 2
- k_weight: bfloat16 [1536, 128], replicated, may hold values from -2 to 2
- v_weight: bfloat16 [1536, 128], replicated, may hold values from -0.15625 to 0.15625
- bias_table: float32 [8, 32, 32], replicated, may hold values from -8 to 8
- buckets: int32 [8, 512], P('dp', 'seq'), may hold values from 0 to 31
- out_weight: bfloat16 [1024, 1536], replicated, may hold values from -1 to 1
Outputs:
- tokens: bfloat16 [8, 512, 1536], P('dp', 'seq')
- mixed: bfloat16 [8, 512, 1536], P('dp', 'seq')
The draws below stay inside these ranges and needn't reach their ends.
All inputs are finite; a program needn't handle non-finite values.
Results may differ from the reference program's by a relative error of at most 0.0091.
Values may be sent and summed in bfloat16 or wider, within the bound.
A program may use at most 128 MiB of HBM per device.

```python
import jax
import jax.numpy as jnp
from jax import lax

C = 1408
KW = 5
D = 1536
H = 8
HD = 128
NB = 32
WINDOWS = 8
POSITIONS = 2048
TOKENS = 512


def shared_channels(factors, loadings):
    mixture = jnp.zeros((WINDOWS, POSITIONS, C), jnp.float32)
    for factor_index in range(8):
        mixture = mixture + factors[:, :, factor_index:factor_index + 1] * loadings[factor_index][None, None, :]
    return mixture * 8.0 ** (-0.5)


def draw_signal(key, part):
    key = jax.random.fold_in(key, 11)
    first = jax.random.fold_in(key, 0)
    second = jax.random.fold_in(key, 1)
    third = jax.random.fold_in(key, 2)
    fifth = jax.random.fold_in(key, 4)
    sixth = jax.random.fold_in(key, 5)
    number = WINDOWS * POSITIONS
    position_index = jnp.arange(number, dtype=jnp.float32) / number
    rising = jnp.exp(jnp.log(3.0) * position_index).reshape(WINDOWS, POSITIONS, 1)
    row_scale = jnp.exp(jax.random.uniform(first, (WINDOWS, POSITIONS, 1), jnp.float32, 0.0, jnp.log(10.0)))
    column_scale = jnp.exp(jax.random.uniform(second, (1, 1, C), jnp.float32, 0.0, jnp.log(10.0)))
    factors = jax.random.normal(fifth, (WINDOWS, POSITIONS, 8), jnp.float32)
    loadings = jax.random.normal(sixth, (8, C), jnp.float32)
    shared = shared_channels(factors, loadings)
    private = jax.random.normal(third, (WINDOWS, POSITIONS, C), jnp.float32)
    noise = jnp.clip(0.6 * private + 0.8 * shared, -4.0, 4.0)
    return (0.2 * rising * row_scale * column_scale * noise).astype(jnp.bfloat16)


def draw_q_weight(key, part):
    key = jax.random.fold_in(key, 21)
    values = jnp.clip(jax.random.normal(key, (D, H * HD), jnp.float32), -5.0, 5.0) * D ** (-0.5)
    return values.astype(jnp.bfloat16)


def draw_k_weight(key, part):
    key = jax.random.fold_in(key, 31)
    values = jnp.clip(jax.random.normal(key, (D, HD), jnp.float32), -5.0, 5.0) * D ** (-0.5)
    return values.astype(jnp.bfloat16)


def plant(entries, stream_key, smallest, high):
    extent = entries.shape
    place = [jax.random.randint(jax.random.fold_in(stream_key, axis), (), 0, extent[axis]) for axis in range(len(extent))]
    entries = entries.at[tuple(place)].set(smallest)
    longest = extent.index(max(extent))
    place[longest] = (place[longest] + 1) % extent[longest]
    return entries.at[tuple(place)].set(high)


def level_of(own_key, extent, shards, least, top_value):
    def one(position, blocks):
        heights = jax.random.uniform(jax.random.fold_in(jax.random.fold_in(own_key, 6), position), (blocks,), jnp.float32, least / len(shards), top_value / len(shards))
        return jnp.repeat(jnp.exp(heights), extent[position] // blocks).reshape((-1,) + (1,) * (len(extent) - position - 1))

    gain = one(*shards[0])
    for cut in shards[1:]:
        gain = gain * one(*cut)
    return gain


def gaussian(key, dims, spread, limit, shards=(), held_as=jnp.bfloat16):
    result = spread * jax.random.normal(key, dims, jnp.float32)
    if shards:
        result = result * level_of(key, dims, shards, -0.22, 0.18)
    return jnp.clip(result, -limit, limit).astype(held_as)


def setup_inputs(seed: int = 0) -> dict:
    key_of = jax.random.split(jax.random.key(seed), 15)
    return {
        "signal": draw_signal(jax.random.fold_in(key_of[14], 71), 0),
        "bases": plant(jax.random.randint(key_of[1], (WINDOWS, POSITIONS), 0, 4), jax.random.fold_in(key_of[1], 1), 0, 3).astype(jnp.int32),
        "base_table": gaussian(key_of[2], (4, C), 1.0, 6.0),
        "conv_weight": gaussian(key_of[3], (KW, C, C), (KW * C) ** -0.5, 0.0625, ((2, 8),)),
        "batch_norm_gain": jnp.clip(1.0 + 0.18 * jax.random.normal(key_of[4], (C,), jnp.float32), 0.1, 1.9),
        "norm_bias": gaussian(key_of[5], (C,), 0.5, 3.0, (), jnp.float32),
        "proj_weight": gaussian(key_of[6], (C, D), C ** -0.5, 0.15625),
        "attn_gain": jnp.clip(1.0 + 0.18 * jax.random.normal(key_of[7], (D,), jnp.float32), 0.1, 1.9),
        "q_weight": draw_q_weight(jax.random.fold_in(key_of[14], 71), 0),
        "k_weight": draw_k_weight(jax.random.fold_in(key_of[14], 71), 0),
        "v_weight": gaussian(key_of[10], (D, HD), D ** -0.5, 0.15625),
        "bias_table": gaussian(key_of[11], (H, NB, NB), 2.0, 8.0, (), jnp.float32),
        "buckets": plant(jax.random.randint(key_of[12], (WINDOWS, TOKENS), 0, NB), jax.random.fold_in(key_of[12], 1), 0, NB - 1).astype(jnp.int32),
        "out_weight": gaussian(key_of[13], (H * HD, D), 0.15, 1.0),
    }


def reference(signal, bases, base_table, conv_weight, batch_norm_gain, norm_bias, proj_weight, attn_gain, q_weight, k_weight, v_weight, bias_table, buckets, out_weight):
    embedded = (signal.astype(jnp.float32) + base_table[bases].astype(jnp.float32)).astype(jnp.bfloat16)
    padded = jnp.pad(embedded, ((0, 0), (2, 2), (0, 0)))

    def convolve(window_rows):
        totals = jnp.zeros((POSITIONS, C), jnp.float32)
        for offset in range(KW):
            totals = totals + jnp.dot(window_rows[offset:offset + POSITIONS], conv_weight[offset], preferred_element_type=jnp.float32)
        return totals
    convolved = lax.map(convolve, padded)
    number = WINDOWS * POSITIONS
    average = lax.optimization_barrier(jnp.sum(convolved, axis=(0, 1))) / number
    centred = convolved - average
    variance = lax.optimization_barrier(jnp.sum(centred * centred, axis=(0, 1))) / number
    normed = jax.nn.gelu(centred * lax.rsqrt(variance + 1e-05) * batch_norm_gain + norm_bias)
    pooled_features = lax.optimization_barrier(jnp.max(normed.reshape(WINDOWS, TOKENS, 4, C), axis=2)).astype(jnp.bfloat16)
    tokens = jnp.dot(pooled_features.reshape(WINDOWS * TOKENS, C), proj_weight, preferred_element_type=jnp.float32).astype(jnp.bfloat16)
    token_float = tokens.astype(jnp.float32)
    normalized = (token_float * lax.rsqrt(lax.optimization_barrier(jnp.mean(token_float * token_float, axis=1, keepdims=True)) + 1e-06) * attn_gain).astype(jnp.bfloat16)
    queries = jnp.dot(normalized, q_weight, preferred_element_type=jnp.float32).astype(jnp.bfloat16).reshape(WINDOWS, TOKENS, H * HD)
    key_rows = jnp.dot(normalized, k_weight, preferred_element_type=jnp.float32).astype(jnp.bfloat16).reshape(WINDOWS, TOKENS, HD)
    value_rows = jnp.dot(normalized, v_weight, preferred_element_type=jnp.float32).astype(jnp.bfloat16).reshape(WINDOWS, TOKENS, HD)
    score_scale = HD ** (-0.5)

    def attend(inputs):
        window_queries, window_keys, window_values, window_buckets = inputs

        def one_head(head):
            head_queries = lax.dynamic_slice_in_dim(window_queries, head * HD, HD, 1)
            scores = jnp.dot(head_queries, window_keys.T, preferred_element_type=jnp.float32) * score_scale
            scores = scores + bias_table[head][window_buckets][:, window_buckets]
            largest = lax.optimization_barrier(jnp.max(scores, axis=1, keepdims=True))
            weights = jnp.exp(scores - largest)
            denominator = lax.optimization_barrier(jnp.sum(weights, axis=1, keepdims=True))
            summed = jnp.dot(weights.astype(jnp.bfloat16), window_values, preferred_element_type=jnp.float32)
            return summed / denominator
        heads_out = lax.map(one_head, jnp.arange(H, dtype=jnp.int32))
        return jnp.transpose(heads_out, (1, 0, 2)).reshape(TOKENS, H * HD).astype(jnp.bfloat16)
    attended = lax.map(attend, (queries, key_rows, value_rows, buckets))
    mixed = jnp.dot(attended.reshape(WINDOWS * TOKENS, H * HD), out_weight, preferred_element_type=jnp.float32).astype(jnp.bfloat16)
    return (tokens.reshape(WINDOWS, TOKENS, D), mixed.reshape(WINDOWS, TOKENS, D))
```

```python
import functools
import math

import jax
import jax.numpy as jnp
from jax import lax
from jax.experimental import pallas as pl
from jax.experimental.pallas import tpu as pltpu
from jax.sharding import PartitionSpec as P


def padded_2(cells, sides, width):
    for axis, dim in sides:
        count = lax.axis_size(axis)
        ends = count - 1
        head = lax.slice_in_dim(cells, 0, width, axis=dim)
        tail = lax.slice_in_dim(cells, cells.shape[dim] - width, cells.shape[dim], axis=dim)
        cells = jnp.concatenate(
            [
                lax.ppermute(tail, axis, [(i, (i + 1) % count) for i in range(ends)]),
                cells,
                lax.ppermute(head, axis, [((i + 1) % count, i) for i in range(ends)]),
            ],
            axis=dim,
        )
    return cells


def add_taps(padded, weights, sequence_length):
    totals = jnp.zeros(padded.shape[:-2] + (sequence_length, weights.shape[2]), jnp.float32)
    for offset in range(weights.shape[0]):
        window_rows = lax.slice_in_dim(
            padded, offset, offset + sequence_length, axis=padded.ndim - 2
        )
        totals = totals + jnp.einsum(
            "...pc,cn->...pn", window_rows, weights[offset], preferred_element_type=jnp.float32
        )
    return totals


def make_block(queries, bias_fragments, score_scale):

    def attend_block(carry, piece, start):
        running_max, denominator, accumulated = carry
        key_rows, value_rows, key_codes = piece
        repeated_base_codes = jnp.concatenate((key_codes, key_codes, key_codes), axis=1)
        scores = (
            jnp.einsum("ihd,jd->hij", queries, key_rows, preferred_element_type=jnp.float32)
            * score_scale
        )
        scores = scores + jnp.einsum(
            "mrz,sz->mrs", bias_fragments, repeated_base_codes, preferred_element_type=jnp.float32
        )
        new_max = jnp.maximum(running_max, jnp.max(scores, axis=2))
        weights = jnp.exp(scores - new_max[:, :, None])
        multiplier = jnp.exp(running_max - new_max)
        denominator = denominator * multiplier + jnp.sum(weights, axis=2)
        accumulated = accumulated * multiplier[:, :, None] + jnp.einsum(
            "hij,jd->hid",
            weights.astype(jnp.bfloat16),
            value_rows,
            preferred_element_type=jnp.float32,
        )
        return (new_max, denominator, accumulated)

    return attend_block


def shards(
    signal,
    bases,
    base_table,
    conv_weight,
    batch_norm_gain,
    norm_bias,
    proj_weight,
    attn_gain,
    q_weight,
    k_weight,
    v_weight,
    bias_table,
    buckets,
    out_weight,
):
    signal_rows = signal[0]
    sequence_length = signal_rows.shape[0]
    channels = signal_rows.shape[1]
    base_onehot = (bases[0][:, None] == jnp.arange(4, dtype=jnp.int32)[None, :]).astype(
        jnp.bfloat16
    )
    embedded = (
        signal_rows.astype(jnp.float32)
        + jnp.dot(base_onehot, base_table, preferred_element_type=jnp.float32)
    ).astype(jnp.bfloat16)
    padded = padded_2(embedded, (("seq", 0),), 2)
    convolved = add_taps(
        padded, lax.all_gather(conv_weight, "dp", axis=2, tiled=True), sequence_length
    )
    number = sequence_length * lax.axis_size("seq") * lax.axis_size("dp")
    totals = lax.psum(jnp.sum(convolved, axis=0), ("dp", "seq"))
    average = totals / number
    centred = convolved - average
    variance = lax.psum(jnp.sum(centred * centred, axis=0), ("dp", "seq")) / number
    normed = jax.nn.gelu(centred * lax.rsqrt(variance + 1e-05) * batch_norm_gain + norm_bias)
    token_count = sequence_length // 4
    pooled_features = jnp.max(normed.reshape(token_count, 4, channels), axis=1).astype(jnp.bfloat16)
    tokens = jnp.dot(pooled_features, proj_weight, preferred_element_type=jnp.float32).astype(
        jnp.bfloat16
    )
    token_float = tokens.astype(jnp.float32)
    normalized = (
        token_float
        * lax.rsqrt(jnp.mean(token_float * token_float, axis=1, keepdims=True) + 1e-06)
        * attn_gain
    ).astype(jnp.bfloat16)
    head_size = k_weight.shape[1]
    head_count = q_weight.shape[1] // head_size
    bucket_count = bias_table.shape[1]
    queries = (
        jnp.dot(normalized, q_weight, preferred_element_type=jnp.float32)
        .astype(jnp.bfloat16)
        .reshape(token_count, head_count, head_size)
    )
    key_rows = jnp.dot(normalized, k_weight, preferred_element_type=jnp.float32).astype(
        jnp.bfloat16
    )
    value_rows = jnp.dot(normalized, v_weight, preferred_element_type=jnp.float32).astype(
        jnp.bfloat16
    )
    bucket_onehot = buckets[0][:, None] == jnp.arange(bucket_count, dtype=jnp.int32)[None, :]
    query_bias = jnp.einsum(
        "vt,wtk->wvk",
        bucket_onehot.astype(jnp.float32),
        bias_table,
        precision=lax.Precision.HIGHEST,
    )
    bias_high = query_bias.astype(jnp.bfloat16)
    remainder = query_bias - bias_high.astype(jnp.float32)
    bias_middle = remainder.astype(jnp.bfloat16)
    lower_bias_part = (remainder - bias_middle.astype(jnp.float32)).astype(jnp.bfloat16)
    bias_fragments = jnp.concatenate((bias_high, bias_middle, lower_bias_part), axis=2)
    key_codes = bucket_onehot.astype(jnp.bfloat16)
    attend_block = make_block(queries, bias_fragments, head_size ** (-0.5))
    initial = (
        jnp.full((head_count, token_count), -1e30, jnp.float32),
        jnp.zeros((head_count, token_count), jnp.float32),
        jnp.zeros((head_count, token_count, head_size), jnp.float32),
    )
    all_rows, all_values, all_codes = (
        lax.all_gather(key_rows, "seq", axis=0, tiled=True),
        lax.all_gather(value_rows, "seq", axis=0, tiled=True),
        lax.all_gather(key_codes, "seq", axis=0, tiled=True),
    )
    key_total = all_rows.shape[0]
    block_rows = math.gcd(512, key_total)
    block_count = key_total // block_rows
    stacked = (
        all_rows.reshape(block_count, block_rows, head_size),
        all_values.reshape(block_count, block_rows, head_size),
        all_codes.reshape(block_count, block_rows, bucket_count),
    )

    def scan_step(carry, piece):
        return (attend_block(carry, piece, 0), None)

    final_state, unused = lax.scan(scan_step, initial, stacked)
    running_max, denominator, accumulated = final_state
    attended = (
        jnp.transpose(accumulated / denominator[:, :, None], (1, 0, 2))
        .reshape(token_count, head_count * head_size)
        .astype(jnp.bfloat16)
    )
    mixed = jnp.dot(attended, out_weight, preferred_element_type=jnp.float32).astype(jnp.bfloat16)
    return (tokens[None], mixed[None])


PLANES = 4
MESH_IDS = pl.DeviceIdType.MESH


def block_kernel(
    cuts,
    planes_ref,
    taps_ref,
    gain_ref,
    shift_ref,
    proj_ref,
    attn_gain_ref,
    q_ref,
    k_ref,
    v_ref,
    table_ref,
    key_codes_ref,
    query_codes_ref,
    out_ref,
    tokens_ref,
    mixed_ref,
    cells,
    taps,
    sums,
    halo,
    edges,
    codes,
    stats,
    staged,
    pooled,
    kv,
    bias,
    proj,
    q_w,
    kv_w,
    out_w,
    attended,
    load_sem,
    halo_send,
    halo_recv,
    edge_send,
    edge_recv,
    code_send,
    code_recv,
    core_send,
    core_recv,
    x_send,
    x_recv,
    pass_send,
    pass_recv,
    tap_send,
    tap_recv,
    tap_pass_send,
    tap_pass_recv,
    stat_send,
    stat_recv,
    pool_send,
    pool_recv,
    kv_send,
    kv_recv,
):
    place = lax.axis_index("dp")
    z = lax.axis_index("seq")
    depth = lax.axis_size("seq")
    core, x, y = place % 2, (place // 2) % 2, place // 4

    def at(y_of, x_of, core_of):
        return (y_of * 2 + x_of) * 2 + core_of

    slots = (
        place,
        at(y, x, 1 - core),
        at(y, 1 - x, core),
        at(y, 1 - x, 1 - core),
    )
    across = at(1 - y, x, core)
    columns = (place, across)
    ring = [(z + step) % depth for step in range(depth)]
    mate = z + 1 - 2 * (z % 2)
    rank = y * depth + z

    def copy(source, target, send, receive, device):
        return pltpu.make_async_remote_copy(
            src_ref=source,
            dst_ref=target,
            send_sem=send,
            recv_sem=receive,
            device_id=device,
            device_id_type=MESH_IDS,
        )

    loads = [
        pltpu.make_async_copy(planes_ref, cells.at[0, 2:6], load_sem.at[0]),
        pltpu.make_async_copy(taps_ref, taps.at[0], load_sem.at[1]),
        pltpu.make_async_copy(proj_ref, proj, load_sem.at[2]),
        pltpu.make_async_copy(q_ref, q_w, load_sem.at[3]),
        pltpu.make_async_copy(k_ref, kv_w.at[:, 0:128], load_sem.at[4]),
        pltpu.make_async_copy(v_ref, kv_w.at[:, 128:256], load_sem.at[5]),
        pltpu.make_async_copy(out_ref, out_w, load_sem.at[6]),
    ]
    for load in loads:
        load.start()

    codes[z] = key_codes_ref[...]
    halo[...] = jnp.zeros_like(halo)

    barrier = pltpu.get_barrier_semaphore()
    partners = [(slots[s], z) for s in (1, 2, 3)] + [(across, z)]
    for step in range(1, depth):
        partners += [(place, ring[step]), (across, ring[step])]
    for partner in partners:
        pl.semaphore_signal(barrier, inc=1, device_id=partner, device_id_type=MESH_IDS)
    loads[0].wait()
    pl.semaphore_wait(barrier, len(partners))

    rows = cells.shape[2]
    to_left = copy(
        cells.at[0, 2:4, 0:16], halo.at[1], halo_send.at[0], halo_recv.at[1], (place, z - 1)
    )
    to_right = copy(
        cells.at[0, 4:6, rows - 16 : rows],
        halo.at[0],
        halo_send.at[1],
        halo_recv.at[0],
        (place, z + 1),
    )
    pl.when(z > 0)(to_left.start)
    pl.when(z < depth - 1)(to_right.start)

    half = (taps.shape[2] // 16 + 1) // 2 * 16
    halves = (slice(0, half), slice(half, taps.shape[2]))

    def by_parity(act):
        for parity in (0, 1):
            pl.when(z % 2 == parity)(functools.partial(act, halves[parity], halves[1 - parity]))

    def own_to_x(i):
        part = cells.at[0, 2:6, :, cuts[i]]
        return copy(
            part, cells.at[2, 2:6, :, cuts[i]], x_send.at[i], x_recv.at[i], (slots[2], z)
        )

    def own_to_core(i):
        part = cells.at[0, 2:6, :, cuts[i]]
        return copy(
            part, cells.at[1, 2:6, :, cuts[i]], core_send.at[i], core_recv.at[i], (slots[1], z)
        )

    def pass_on(i):
        part = cells.at[2, 2:6, :, cuts[i]]
        return copy(
            part, cells.at[3, 2:6, :, cuts[i]], pass_send.at[i], pass_recv.at[i], (slots[1], z)
        )

    def taps_across(i, mine):
        return copy(
            taps.at[0, :, mine, cuts[i]],
            taps.at[1, :, mine, cuts[i]],
            tap_send.at[i],
            tap_recv.at[i],
            (across, z),
        )

    def taps_pass(i, part):
        return copy(
            taps.at[1, :, part, cuts[i]],
            taps.at[1, :, part, cuts[i]],
            tap_pass_send.at[i],
            tap_pass_recv.at[i],
            (place, mate),
        )

    number = len(cuts)
    for i in range(number):
        own_to_x(i).start()
        if i == 0:
            loads[1].wait()
        by_parity(lambda mine, other: taps_across(i, mine).start())
        own_to_core(i).start()

    code_copies = [
        copy(codes.at[z], codes.at[z], code_send.at[s], code_recv.at[s], (place, ring[s]))
        for s in range(1, depth)
    ]
    for item in code_copies:
        item.start()

    pl.when(z > 0)(lambda: copy(
        cells.at[0, 2:4, 0:16], halo.at[0], halo_send.at[0], halo_recv.at[0], (place, z - 1)
    ).wait_recv())
    pl.when(z < depth - 1)(lambda: copy(
        cells.at[0, 2:4, 0:16], halo.at[1], halo_send.at[0], halo_recv.at[1], (place, z + 1)
    ).wait_recv())
    row = lax.broadcasted_iota(jnp.int32, (16, 1), 0)
    before = halo[0].astype(jnp.float32)
    after = halo[1].astype(jnp.float32)
    edge = jnp.where(row == 0, before[0, 15:16], 0.0)
    edge = jnp.where(row == 1, before[1, 15:16], edge)
    edge = jnp.where(row == 2, after[0, 0:1], edge)
    edge = jnp.where(row == 3, after[1, 0:1], edge)
    edges[0] = edge.astype(jnp.bfloat16)
    edge_copies = [
        copy(edges.at[0], edges.at[s], edge_send.at[s], edge_recv.at[s], (slots[s], z))
        for s in (1, 2, 3)
    ]
    for item in edge_copies:
        item.start()

    for item in code_copies:
        item.wait_recv()
    heads = table_ref.shape[0]

    def add_bias(head, carry):
        table = table_ref[head]
        rest = table
        for part in range(3):
            piece = rest.astype(jnp.bfloat16)
            rest = rest - piece.astype(jnp.float32)
            of_query = jnp.dot(
                query_codes_ref[...], piece, preferred_element_type=jnp.float32
            ).astype(jnp.bfloat16)
            for s in range(depth):
                block = jnp.dot(of_query, codes[s], preferred_element_type=jnp.float32)
                columns_of = slice(s * 128, (s + 1) * 128)
                if part == 0:
                    bias[head, :, columns_of] = block
                else:
                    bias[head, :, columns_of] += block
        return carry

    lax.fori_loop(0, heads, add_bias, 0)
    for item in edge_copies:
        item.wait_recv()

    def convolve(i):
        cut = cuts[i]

        def one_window(slot, carry):
            fringe = edges[slot, :, cut].astype(jnp.float32)
            line = lax.broadcasted_iota(jnp.int32, (rows, 1), 0)
            for target, source, edge_row in ((0, 4, 0), (1, 5, 1), (6, 2, 2), (7, 3, 3)):
                values = cells[slot, source, :, cut].astype(jnp.float32)
                if target < 2:
                    moved, end = pltpu.roll(values, 1, 0), 0
                else:
                    moved, end = pltpu.roll(values, rows - 1, 0), rows - 1
                cells[slot, target, :, cut] = jnp.where(
                    line == end, fringe[edge_row : edge_row + 1], moved
                ).astype(jnp.bfloat16)
            for side in range(2):
                total = None
                for t in range(taps.shape[1]):
                    part = cells[slot, t : t + PLANES, :, cut].reshape(PLANES * rows, -1)
                    term = lax.dot_general(
                        part,
                        taps[side, t, :, cut],
                        (((1,), (1,)), ((), ())),
                        preferred_element_type=jnp.float32,
                    )
                    total = term if total is None else total + term
                if i == 0:
                    sums[slot, side] = total
                else:
                    sums[slot, side] += total
            return carry

        lax.fori_loop(0, 4, one_window, 0)

    def arrive(i):
        own_to_core(i).wait_recv()
        pass_on(i).wait_recv()
        by_parity(lambda mine, other: taps_pass(i, other).wait_recv())

    for i in range(number):
        own_to_x(i).wait_recv()
        pass_on(i).start()
        by_parity(lambda mine, other: taps_across(i, mine).wait_recv())
        by_parity(lambda mine, other: taps_pass(i, mine).start())
        if i:
            arrive(i - 1)
            convolve(i - 1)
    arrive(number - 1)
    convolve(number - 1)

    local = 4 * PLANES * rows
    line = lax.broadcasted_iota(jnp.int32, (8, 1), 0)
    for side, owner_y in ((0, y), (1, 1 - y)):
        mean = sum(jnp.sum(sums[s, side], axis=0, keepdims=True) for s in range(4)) / local
        squares = sum(
            jnp.sum(jnp.square(sums[s, side] - mean), axis=0, keepdims=True) for s in range(4)
        )
        stats[rank, owner_y] = jnp.where(line == 0, mean, jnp.where(line == 1, squares, 0.0))
    stat_copies = []
    for dy, y_to in ((0, y), (1, 1 - y)):
        for step in range(depth):
            if dy or step:
                n = dy * depth + step
                stat_copies.append(
                    copy(
                        stats.at[rank],
                        stats.at[rank],
                        stat_send.at[n],
                        stat_recv.at[n],
                        (at(y_to, x, core), ring[step]),
                    )
                )
    for item in stat_copies:
        item.start()
    for item in stat_copies:
        item.wait_recv()
    ranks = 2 * depth

    def normalise(side, owner_y, column):
        means = [stats[r, owner_y, 0:1] for r in range(ranks)]
        mean = sum(means) / ranks
        squares = sum(stats[r, owner_y, 1:2] for r in range(ranks))
        squares = squares + local * sum(jnp.square(m - mean) for m in means)
        factor = lax.rsqrt(squares / (local * ranks) + 1e-05) * gain_ref[column]
        shift = shift_ref[column]

        def activate(slot):
            cube = sums[slot, side].reshape(PLANES, rows, -1)
            cube = (cube - mean) * factor + shift
            top, low = jnp.max(cube, axis=0), jnp.min(cube, axis=0)
            return jnp.maximum(jax.nn.gelu(top), jax.nn.gelu(low)).astype(jnp.bfloat16)

        return activate

    activations = [normalise(0, y, columns[0]), normalise(1, 1 - y, columns[1])]
    pool_copies = []
    for slot in (3, 2, 1):
        for side in (0, 1):
            staged[slot, side] = activations[side](slot)
            item = copy(
                staged.at[slot, side],
                pooled.at[columns[side]],
                pool_send.at[slot, side],
                pool_recv.at[slot, side],
                (slots[slot], z),
            )
            item.start()
            pool_copies.append(item)
    for side in (0, 1):
        pooled[columns[side]] = activations[side](0)
    for load in loads[2:]:
        load.wait()
    for item in pool_copies:
        item.wait_recv()

    share = pooled.shape[2]
    total = None
    for d in range(pooled.shape[0]):
        term = jnp.dot(
            pooled[d], proj[d * share : (d + 1) * share], preferred_element_type=jnp.float32
        )
        total = term if total is None else total + term
    tokens = total.astype(jnp.bfloat16)
    tokens_ref[...] = tokens
    wide = tokens.astype(jnp.float32)
    normalized = (
        wide
        * lax.rsqrt(jnp.mean(wide * wide, axis=1, keepdims=True) + 1e-06)
        * attn_gain_ref[...]
    ).astype(jnp.bfloat16)
    kv[z] = jnp.dot(normalized, kv_w[...], preferred_element_type=jnp.float32).astype(
        jnp.bfloat16
    )
    kv_copies = [
        copy(kv.at[z], kv.at[z], kv_send.at[s], kv_recv.at[s], (place, ring[s]))
        for s in range(1, depth)
    ]
    for item in kv_copies:
        item.start()
    queries = jnp.dot(normalized, q_w[...], preferred_element_type=jnp.float32).astype(
        jnp.bfloat16
    )
    for item in kv_copies:
        item.wait_recv()
    keys = kv[:, :, 0:128].reshape(depth * rows, 128)
    values = kv[:, :, 128:256].reshape(depth * rows, 128)
    for head in range(heads):
        lanes = slice(head * 128, (head + 1) * 128)
        scores = lax.dot_general(
            queries[:, lanes],
            keys,
            (((1,), (1,)), ((), ())),
            preferred_element_type=jnp.float32,
        )
        scores = scores * (128**-0.5) + bias[head]
        weights = jnp.exp(scores - jnp.max(scores, axis=1, keepdims=True))
        denominator = jnp.sum(weights, axis=1, keepdims=True)
        summed = jnp.dot(weights.astype(jnp.bfloat16), values, preferred_element_type=jnp.float32)
        attended[:, lanes] = (summed / denominator).astype(jnp.bfloat16)
    mixed_ref[...] = jnp.dot(
        attended[...], out_w[...], preferred_element_type=jnp.float32
    ).astype(jnp.bfloat16)

    pl.when(z > 0)(to_left.wait_send)
    pl.when(z < depth - 1)(to_right.wait_send)
    for i in range(number):
        own_to_x(i).wait_send()
        own_to_core(i).wait_send()
        pass_on(i).wait_send()
        by_parity(lambda mine, other: taps_across(i, mine).wait_send())
        by_parity(lambda mine, other: taps_pass(i, mine).wait_send())
    for item in code_copies + edge_copies + stat_copies + pool_copies + kv_copies:
        item.wait_send()


def fused_shards(
    signal,
    bases,
    base_table,
    conv_weight,
    batch_norm_gain,
    norm_bias,
    proj_weight,
    attn_gain,
    q_weight,
    k_weight,
    v_weight,
    bias_table,
    buckets,
    out_weight,
):
    positions, channels = signal.shape[1:]
    rows = positions // PLANES
    devices, depth = lax.axis_size("dp"), lax.axis_size("seq")
    width = conv_weight.shape[0]
    share = conv_weight.shape[2]
    heads, classes = bias_table.shape[:2]
    model = proj_weight.shape[1]
    base_onehot = (bases[0][:, None] == jnp.arange(4, dtype=jnp.int32)[None, :]).astype(
        jnp.bfloat16
    )
    embedded = (
        signal[0].astype(jnp.float32)
        + jnp.dot(base_onehot, base_table, preferred_element_type=jnp.float32)
    ).astype(jnp.bfloat16)
    planes = jnp.transpose(embedded.reshape(rows, PLANES, channels), (1, 0, 2))
    taps = jnp.transpose(conv_weight, (0, 2, 1))
    kinds = jnp.arange(classes, dtype=jnp.int32)
    query_codes = (buckets[0][:, None] == kinds[None, :]).astype(jnp.bfloat16)
    key_codes = (kinds[:, None] == buckets[0][None, :]).astype(jnp.bfloat16)
    cuts = tuple(
        slice(start, min(start + 256, channels)) for start in range(0, channels, 256)
    )
    number = len(cuts)
    vmem = pl.BlockSpec(memory_space=pltpu.VMEM)
    anywhere = pl.BlockSpec(memory_space=pl.ANY)
    dma = pltpu.SemaphoreType.DMA
    narrow, wide = jnp.bfloat16, jnp.float32
    tokens, mixed = pl.pallas_call(
        functools.partial(block_kernel, cuts),
        out_shape=[jax.ShapeDtypeStruct((rows, model), narrow)] * 2,
        in_specs=[
            anywhere,
            anywhere,
            vmem,
            vmem,
            anywhere,
            vmem,
            anywhere,
            anywhere,
            anywhere,
            vmem,
            vmem,
            vmem,
            anywhere,
        ],
        out_specs=[vmem, vmem],
        scratch_shapes=[
            pltpu.VMEM((4, PLANES + width - 1, rows, channels), narrow),
            pltpu.VMEM((2, width, share, channels), narrow),
            pltpu.VMEM((4, 2, positions, share), wide),
            pltpu.VMEM((2, 2, 16, channels), narrow),
            pltpu.VMEM((4, 16, channels), narrow),
            pltpu.VMEM((depth, classes, rows), narrow),
            pltpu.VMEM((2 * depth, 2, 8, share), wide),
            pltpu.VMEM((4, 2, rows, share), narrow),
            pltpu.VMEM((devices, rows, share), narrow),
            pltpu.VMEM((depth, rows, 256), narrow),
            pltpu.VMEM((heads, rows, depth * rows), wide),
            pltpu.VMEM(proj_weight.shape, narrow),
            pltpu.VMEM(q_weight.shape, narrow),
            pltpu.VMEM((model, 256), narrow),
            pltpu.VMEM(out_weight.shape, narrow),
            pltpu.VMEM((rows, q_weight.shape[1]), narrow),
            dma((7,)),
            dma((2,)),
            dma((2,)),
            dma((4,)),
            dma((4,)),
            dma((depth,)),
            dma((depth,)),
            dma((number,)),
            dma((number,)),
            dma((number,)),
            dma((number,)),
            dma((number,)),
            dma((number,)),
            dma((number,)),
            dma((number,)),
            dma((number,)),
            dma((number,)),
            dma((2 * depth,)),
            dma((2 * depth,)),
            dma((4, 2)),
            dma((4, 2)),
            dma((depth,)),
            dma((depth,)),
        ],
        compiler_params=pltpu.CompilerParams(
            collective_id=0, has_side_effects=True, vmem_limit_bytes=52 * 1024 * 1024
        ),
        cost_estimate=pl.CostEstimate(
            flops=12_000_000_000, bytes_accessed=20_000_000, transcendentals=4_000_000
        ),
    )(
        planes,
        taps,
        batch_norm_gain.reshape(devices, 1, share),
        norm_bias.reshape(devices, 1, share),
        proj_weight,
        attn_gain[None],
        q_weight,
        k_weight,
        v_weight,
        bias_table,
        key_codes,
        query_codes,
        out_weight,
    )
    return (tokens[None], mixed[None])


def solution(mesh):
    placed = (
        P("dp", "seq", None),
        P("dp", "seq"),
        P(),
        P(None, None, "dp"),
        P(),
        P(),
        P(),
        P(),
        P(),
        P(),
        P(),
        P(),
        P("dp", "seq"),
        P(),
    )
    whole_cube = mesh.shape["dp"] == 8 and mesh.shape["seq"] == 4
    return jax.shard_map(
        fused_shards if whole_cube else shards,
        mesh=mesh,
        in_specs=placed,
        out_specs=(P("dp", "seq", None), P("dp", "seq", None)),
        check_vma=False,
    )
```

```python
import functools
import math

import jax
import jax.numpy as jnp
from jax import lax
from jax.experimental import pallas as pl
from jax.experimental.pallas import tpu as pltpu
from jax.sharding import PartitionSpec as P


def padded_2(cells, sides, width):
    for axis, dim in sides:
        count = lax.axis_size(axis)
        ends = count - 1
        head = lax.slice_in_dim(cells, 0, width, axis=dim)
        tail = lax.slice_in_dim(cells, cells.shape[dim] - width, cells.shape[dim], axis=dim)
        cells = jnp.concatenate(
            [
                lax.ppermute(tail, axis, [(i, (i + 1) % count) for i in range(ends)]),
                cells,
                lax.ppermute(head, axis, [((i + 1) % count, i) for i in range(ends)]),
            ],
            axis=dim,
        )
    return cells


def add_taps(padded, weights, sequence_length):
    totals = jnp.zeros(padded.shape[:-2] + (sequence_length, weights.shape[2]), jnp.float32)
    for offset in range(weights.shape[0]):
        window_rows = lax.slice_in_dim(
            padded, offset, offset + sequence_length, axis=padded.ndim - 2
        )
        totals = totals + jnp.einsum(
            "...pc,cn->...pn", window_rows, weights[offset], preferred_element_type=jnp.float32
        )
    return totals


def make_block(queries, bias_fragments, score_scale):

    def attend_block(carry, piece, start):
        running_max, denominator, accumulated = carry
        key_rows, value_rows, key_codes = piece
        repeated_base_codes = jnp.concatenate((key_codes, key_codes, key_codes), axis=1)
        scores = (
            jnp.einsum("ihd,jd->hij", queries, key_rows, preferred_element_type=jnp.float32)
            * score_scale
        )
        scores = scores + jnp.einsum(
            "mrz,sz->mrs", bias_fragments, repeated_base_codes, preferred_element_type=jnp.float32
        )
        new_max = jnp.maximum(running_max, jnp.max(scores, axis=2))
        weights = jnp.exp(scores - new_max[:, :, None])
        multiplier = jnp.exp(running_max - new_max)
        denominator = denominator * multiplier + jnp.sum(weights, axis=2)
        accumulated = accumulated * multiplier[:, :, None] + jnp.einsum(
            "hij,jd->hid",
            weights.astype(jnp.bfloat16),
            value_rows,
            preferred_element_type=jnp.float32,
        )
        return (new_max, denominator, accumulated)

    return attend_block


def shards(
    signal,
    bases,
    base_table,
    conv_weight,
    batch_norm_gain,
    norm_bias,
    proj_weight,
    attn_gain,
    q_weight,
    k_weight,
    v_weight,
    bias_table,
    buckets,
    out_weight,
):
    signal_rows = signal[0]
    sequence_length = signal_rows.shape[0]
    channels = signal_rows.shape[1]
    base_onehot = (bases[0][:, None] == jnp.arange(4, dtype=jnp.int32)[None, :]).astype(
        jnp.bfloat16
    )
    embedded = (
        signal_rows.astype(jnp.float32)
        + jnp.dot(base_onehot, base_table, preferred_element_type=jnp.float32)
    ).astype(jnp.bfloat16)
    padded = padded_2(embedded, (("seq", 0),), 2)
    convolved = add_taps(
        padded, lax.all_gather(conv_weight, "dp", axis=2, tiled=True), sequence_length
    )
    number = sequence_length * lax.axis_size("seq") * lax.axis_size("dp")
    totals = lax.psum(jnp.sum(convolved, axis=0), ("dp", "seq"))
    average = totals / number
    centred = convolved - average
    variance = lax.psum(jnp.sum(centred * centred, axis=0), ("dp", "seq")) / number
    normed = jax.nn.gelu(centred * lax.rsqrt(variance + 1e-05) * batch_norm_gain + norm_bias)
    token_count = sequence_length // 4
    pooled_features = jnp.max(normed.reshape(token_count, 4, channels), axis=1).astype(jnp.bfloat16)
    tokens = jnp.dot(pooled_features, proj_weight, preferred_element_type=jnp.float32).astype(
        jnp.bfloat16
    )
    token_float = tokens.astype(jnp.float32)
    normalized = (
        token_float
        * lax.rsqrt(jnp.mean(token_float * token_float, axis=1, keepdims=True) + 1e-06)
        * attn_gain
    ).astype(jnp.bfloat16)
    head_size = k_weight.shape[1]
    head_count = q_weight.shape[1] // head_size
    bucket_count = bias_table.shape[1]
    queries = (
        jnp.dot(normalized, q_weight, preferred_element_type=jnp.float32)
        .astype(jnp.bfloat16)
        .reshape(token_count, head_count, head_size)
    )
    key_rows = jnp.dot(normalized, k_weight, preferred_element_type=jnp.float32).astype(
        jnp.bfloat16
    )
    value_rows = jnp.dot(normalized, v_weight, preferred_element_type=jnp.float32).astype(
        jnp.bfloat16
    )
    bucket_onehot = buckets[0][:, None] == jnp.arange(bucket_count, dtype=jnp.int32)[None, :]
    query_bias = jnp.einsum(
        "vt,wtk->wvk",
        bucket_onehot.astype(jnp.float32),
        bias_table,
        precision=lax.Precision.HIGHEST,
    )
    bias_high = query_bias.astype(jnp.bfloat16)
    remainder = query_bias - bias_high.astype(jnp.float32)
    bias_middle = remainder.astype(jnp.bfloat16)
    lower_bias_part = (remainder - bias_middle.astype(jnp.float32)).astype(jnp.bfloat16)
    bias_fragments = jnp.concatenate((bias_high, bias_middle, lower_bias_part), axis=2)
    key_codes = bucket_onehot.astype(jnp.bfloat16)
    attend_block = make_block(queries, bias_fragments, head_size ** (-0.5))
    initial = (
        jnp.full((head_count, token_count), -1e30, jnp.float32),
        jnp.zeros((head_count, token_count), jnp.float32),
        jnp.zeros((head_count, token_count, head_size), jnp.float32),
    )
    all_rows, all_values, all_codes = (
        lax.all_gather(key_rows, "seq", axis=0, tiled=True),
        lax.all_gather(value_rows, "seq", axis=0, tiled=True),
        lax.all_gather(key_codes, "seq", axis=0, tiled=True),
    )
    key_total = all_rows.shape[0]
    block_rows = math.gcd(512, key_total)
    block_count = key_total // block_rows
    stacked = (
        all_rows.reshape(block_count, block_rows, head_size),
        all_values.reshape(block_count, block_rows, head_size),
        all_codes.reshape(block_count, block_rows, bucket_count),
    )

    def scan_step(carry, piece):
        return (attend_block(carry, piece, 0), None)

    final_state, unused = lax.scan(scan_step, initial, stacked)
    running_max, denominator, accumulated = final_state
    attended = (
        jnp.transpose(accumulated / denominator[:, :, None], (1, 0, 2))
        .reshape(token_count, head_count * head_size)
        .astype(jnp.bfloat16)
    )
    mixed = jnp.dot(attended, out_weight, preferred_element_type=jnp.float32).astype(jnp.bfloat16)
    return (tokens[None], mixed[None])


PLANES = 4
SHARED_CUTS = 2
MESH_IDS = pl.DeviceIdType.MESH


def block_kernel(
    cuts,
    signal_ref,
    bases_ref,
    base_table_ref,
    taps_ref,
    gain_ref,
    shift_ref,
    proj_ref,
    attn_gain_ref,
    q_ref,
    k_ref,
    v_ref,
    table_ref,
    buckets_ref,
    out_ref,
    tokens_ref,
    mixed_ref,
    raw,
    spread,
    cells,
    taps,
    sums,
    halo,
    edges,
    codes,
    stats,
    staged,
    pooled,
    kv,
    bias,
    proj,
    q_w,
    kv_w,
    out_w,
    attended,
    load_sem,
    halo_send,
    halo_recv,
    edge_send,
    edge_recv,
    code_send,
    code_recv,
    core_send,
    core_recv,
    x_send,
    x_recv,
    pass_send,
    pass_recv,
    tap_send,
    tap_recv,
    tap_pass_send,
    tap_pass_recv,
    stat_send,
    stat_recv,
    pool_send,
    pool_recv,
    kv_send,
    kv_recv,
):
    place = lax.axis_index("dp")
    z = lax.axis_index("seq")
    depth = lax.axis_size("seq")
    core, x, y = place % 2, (place // 2) % 2, place // 4

    def at(y_of, x_of, core_of):
        return (y_of * 2 + x_of) * 2 + core_of

    slots = (
        place,
        at(y, x, 1 - core),
        at(y, 1 - x, core),
        at(y, 1 - x, 1 - core),
    )
    across = at(1 - y, x, core)
    columns = (place, across)
    ring = [(z + step) % depth for step in range(depth)]
    mate = z + 1 - 2 * (z % 2)
    rank = y * depth + z

    def copy(source, target, send, receive, device):
        return pltpu.make_async_remote_copy(
            src_ref=source,
            dst_ref=target,
            send_sem=send,
            recv_sem=receive,
            device_id=device,
            device_id_type=MESH_IDS,
        )

    loads = [
        pltpu.make_async_copy(taps_ref, taps.at[0], load_sem.at[1]),
        pltpu.make_async_copy(signal_ref, raw, load_sem.at[0]),
        pltpu.make_async_copy(proj_ref, proj, load_sem.at[2]),
        pltpu.make_async_copy(q_ref, q_w, load_sem.at[3]),
        pltpu.make_async_copy(k_ref, kv_w.at[:, 0:128], load_sem.at[4]),
        pltpu.make_async_copy(v_ref, kv_w.at[:, 128:256], load_sem.at[5]),
        pltpu.make_async_copy(out_ref, out_w, load_sem.at[6]),
    ]
    for load in loads:
        load.start()

    kinds = lax.broadcasted_iota(jnp.int32, codes.shape[1:], 0)
    own_codes = (kinds == buckets_ref[...]).astype(jnp.float32)
    codes[z] = own_codes.astype(jnp.bfloat16)
    query_codes = jnp.transpose(own_codes).astype(jnp.bfloat16)
    halo[...] = jnp.zeros_like(halo)

    barrier = pltpu.get_barrier_semaphore()
    partners = [(slots[s], z) for s in (1, 2, 3)] + [(across, z)]
    for step in range(1, depth):
        partners += [(place, ring[step]), (across, ring[step])]
    for partner in partners:
        pl.semaphore_signal(barrier, inc=1, device_id=partner, device_id_type=MESH_IDS)
    pl.semaphore_wait(barrier, len(partners))

    rows = cells.shape[2]
    half = (taps.shape[2] // 16 + 1) // 2 * 16
    halves = (slice(0, half), slice(half, taps.shape[2]))

    def by_parity(act):
        for parity in (0, 1):
            pl.when(z % 2 == parity)(functools.partial(act, halves[parity], halves[1 - parity]))

    def each_across(i, act):
        if i < SHARED_CUTS:
            by_parity(lambda mine, other: act(taps_across(i, mine)))
        else:
            act(taps_across(i, slice(0, taps.shape[2])))

    def each_pass(i, act, received):
        if i < SHARED_CUTS:
            by_parity(lambda mine, other: act(taps_pass(i, other if received else mine)))

    def own_to_x(i):
        part = cells.at[0, 2:6, :, cuts[i]]
        return copy(
            part, cells.at[2, 2:6, :, cuts[i]], x_send.at[i], x_recv.at[i], (slots[2], z)
        )

    def own_to_core(i):
        part = cells.at[0, 2:6, :, cuts[i]]
        return copy(
            part, cells.at[1, 2:6, :, cuts[i]], core_send.at[i], core_recv.at[i], (slots[1], z)
        )

    def pass_on(i):
        part = cells.at[2, 2:6, :, cuts[i]]
        return copy(
            part, cells.at[3, 2:6, :, cuts[i]], pass_send.at[i], pass_recv.at[i], (slots[1], z)
        )

    def taps_across(i, mine):
        return copy(
            taps.at[0, :, mine, cuts[i]],
            taps.at[1, :, mine, cuts[i]],
            tap_send.at[i],
            tap_recv.at[i],
            (across, z),
        )

    def taps_pass(i, part):
        return copy(
            taps.at[1, :, part, cuts[i]],
            taps.at[1, :, part, cuts[i]],
            tap_pass_send.at[i],
            tap_pass_recv.at[i],
            (place, mate),
        )

    number = len(cuts)
    loads[0].wait()
    for i in range(number):
        each_across(i, lambda item: item.start())
    base_kinds = lax.broadcasted_iota(jnp.int32, (8, raw.shape[0]), 0)
    base_codes = jnp.transpose((base_kinds == bases_ref[...]).astype(jnp.float32))
    base_codes = base_codes[:, 0:4].astype(jnp.bfloat16)
    loads[1].wait()
    for i in range(number):
        cut = cuts[i]
        embedded = raw[:, cut].astype(jnp.float32) + jnp.dot(
            base_codes, base_table_ref[:, cut], preferred_element_type=jnp.float32
        )
        for start in range(cut.start, cut.stop, 128):
            spread[start // 128] = embedded[:, start - cut.start : start - cut.start + 128]
            for plane in range(PLANES):
                cells[0, 2 + plane, :, start : start + 128] = spread[
                    start // 128, pl.ds(plane, rows, stride=PLANES), :
                ].astype(jnp.bfloat16)
        own_to_x(i).start()
        own_to_core(i).start()

    to_left = copy(
        cells.at[0, 2:4, 0:16], halo.at[1], halo_send.at[0], halo_recv.at[1], (place, z - 1)
    )
    to_right = copy(
        cells.at[0, 4:6, rows - 16 : rows],
        halo.at[0],
        halo_send.at[1],
        halo_recv.at[0],
        (place, z + 1),
    )
    pl.when(z > 0)(to_left.start)
    pl.when(z < depth - 1)(to_right.start)

    code_copies = [
        copy(codes.at[z], codes.at[z], code_send.at[s], code_recv.at[s], (place, ring[s]))
        for s in range(1, depth)
    ]
    for item in code_copies:
        item.start()

    pl.when(z > 0)(lambda: copy(
        cells.at[0, 2:4, 0:16], halo.at[0], halo_send.at[0], halo_recv.at[0], (place, z - 1)
    ).wait_recv())
    pl.when(z < depth - 1)(lambda: copy(
        cells.at[0, 2:4, 0:16], halo.at[1], halo_send.at[0], halo_recv.at[1], (place, z + 1)
    ).wait_recv())
    row = lax.broadcasted_iota(jnp.int32, (16, 1), 0)
    before = halo[0].astype(jnp.float32)
    after = halo[1].astype(jnp.float32)
    edge = jnp.where(row == 0, before[0, 15:16], 0.0)
    edge = jnp.where(row == 1, before[1, 15:16], edge)
    edge = jnp.where(row == 2, after[0, 0:1], edge)
    edge = jnp.where(row == 3, after[1, 0:1], edge)
    edges[0] = edge.astype(jnp.bfloat16)
    edge_copies = [
        copy(edges.at[0], edges.at[s], edge_send.at[s], edge_recv.at[s], (slots[s], z))
        for s in (1, 2, 3)
    ]
    for item in edge_copies:
        item.start()

    for item in code_copies:
        item.wait_recv()
    heads = table_ref.shape[0]

    def add_bias(head, carry):
        table = table_ref[head]
        rest = table
        for part in range(3):
            piece = rest.astype(jnp.bfloat16)
            rest = rest - piece.astype(jnp.float32)
            of_query = jnp.dot(
                query_codes, piece, preferred_element_type=jnp.float32
            ).astype(jnp.bfloat16)
            for s in range(depth):
                block = jnp.dot(of_query, codes[s], preferred_element_type=jnp.float32)
                columns_of = slice(s * 128, (s + 1) * 128)
                if part == 0:
                    bias[head, :, columns_of] = block
                else:
                    bias[head, :, columns_of] += block
        return carry

    lax.fori_loop(0, heads, add_bias, 0)
    for item in edge_copies:
        item.wait_recv()

    def convolve(i, first, last, sides, shifts):
        cut = cuts[i]

        def one_window(slot, carry):
            fringe = edges[slot, :, cut].astype(jnp.float32)
            line = lax.broadcasted_iota(jnp.int32, (rows, 1), 0)
            for target, source, edge_row in shifts:
                values = cells[slot, source, :, cut].astype(jnp.float32)
                if target < 2:
                    moved, end = pltpu.roll(values, 1, 0), 0
                else:
                    moved, end = pltpu.roll(values, rows - 1, 0), rows - 1
                cells[slot, target, :, cut] = jnp.where(
                    line == end, fringe[edge_row : edge_row + 1], moved
                ).astype(jnp.bfloat16)
            for side in sides:
                total = None
                for t in range(taps.shape[1]):
                    part = cells[slot, t : t + PLANES, :, cut].reshape(PLANES * rows, -1)
                    term = lax.dot_general(
                        part,
                        taps[side, t, :, cut],
                        (((1,), (1,)), ((), ())),
                        preferred_element_type=jnp.float32,
                    )
                    total = term if total is None else total + term
                if i == 0:
                    sums[slot, side] = total
                else:
                    sums[slot, side] += total
            return carry

        lax.fori_loop(first, last, one_window, 0)

    def arrive(i):
        pass_on(i).wait_recv()
        each_pass(i, lambda item: item.wait_recv(), True)

    shifted = ((0, 4, 0), (1, 5, 1), (6, 2, 2), (7, 3, 3))
    for i in range(number):
        own_to_core(i).wait_recv()
        convolve(i, 0, 2, (0,), shifted)
    for i in range(number):
        own_to_x(i).wait_recv()
        pass_on(i).start()
        each_across(i, lambda item: item.wait_recv())
        each_pass(i, lambda item: item.start(), False)
        if i:
            arrive(i - 1)
            convolve(i - 1, 2, 4, (0, 1), shifted)
            convolve(i - 1, 0, 2, (1,), ())
    arrive(number - 1)
    convolve(number - 1, 2, 4, (0, 1), shifted)
    convolve(number - 1, 0, 2, (1,), ())

    local = 4 * PLANES * rows
    line = lax.broadcasted_iota(jnp.int32, (8, 1), 0)
    for side, owner_y in ((0, y), (1, 1 - y)):
        mean = sum(jnp.sum(sums[s, side], axis=0, keepdims=True) for s in range(4)) / local
        squares = sum(
            jnp.sum(jnp.square(sums[s, side] - mean), axis=0, keepdims=True) for s in range(4)
        )
        stats[rank, owner_y] = jnp.where(line == 0, mean, jnp.where(line == 1, squares, 0.0))
    stat_copies = []
    for dy, y_to in ((0, y), (1, 1 - y)):
        for step in range(depth):
            if dy or step:
                n = dy * depth + step
                stat_copies.append(
                    copy(
                        stats.at[rank],
                        stats.at[rank],
                        stat_send.at[n],
                        stat_recv.at[n],
                        (at(y_to, x, core), ring[step]),
                    )
                )
    for item in stat_copies:
        item.start()
    for item in stat_copies:
        item.wait_recv()
    ranks = 2 * depth

    def normalise(side, owner_y, column):
        means = [stats[r, owner_y, 0:1] for r in range(ranks)]
        mean = sum(means) / ranks
        squares = sum(stats[r, owner_y, 1:2] for r in range(ranks))
        squares = squares + local * sum(jnp.square(m - mean) for m in means)
        factor = lax.rsqrt(squares / (local * ranks) + 1e-05) * gain_ref[column]
        shift = shift_ref[column]

        def activate(slot):
            cube = sums[slot, side].reshape(PLANES, rows, -1)
            cube = (cube - mean) * factor + shift
            top, low = jnp.max(cube, axis=0), jnp.min(cube, axis=0)
            return jnp.maximum(jax.nn.gelu(top), jax.nn.gelu(low)).astype(jnp.bfloat16)

        return activate

    activations = [normalise(0, y, columns[0]), normalise(1, 1 - y, columns[1])]
    pool_copies = []
    for slot in (3, 2, 1):
        for side in (0, 1):
            staged[slot, side] = activations[side](slot)
            item = copy(
                staged.at[slot, side],
                pooled.at[columns[side]],
                pool_send.at[slot, side],
                pool_recv.at[slot, side],
                (slots[slot], z),
            )
            item.start()
            pool_copies.append(item)
    for side in (0, 1):
        pooled[columns[side]] = activations[side](0)
    for load in loads[2:]:
        load.wait()
    for item in pool_copies:
        item.wait_recv()

    share = pooled.shape[2]
    total = None
    for d in range(pooled.shape[0]):
        term = jnp.dot(
            pooled[d], proj[d * share : (d + 1) * share], preferred_element_type=jnp.float32
        )
        total = term if total is None else total + term
    tokens = total.astype(jnp.bfloat16)
    tokens_ref[...] = tokens
    wide = tokens.astype(jnp.float32)
    normalized = (
        wide
        * lax.rsqrt(jnp.mean(wide * wide, axis=1, keepdims=True) + 1e-06)
        * attn_gain_ref[...]
    ).astype(jnp.bfloat16)
    kv[z] = jnp.dot(normalized, kv_w[...], preferred_element_type=jnp.float32).astype(
        jnp.bfloat16
    )
    kv_copies = [
        copy(kv.at[z], kv.at[z], kv_send.at[s], kv_recv.at[s], (place, ring[s]))
        for s in range(1, depth)
    ]
    for item in kv_copies:
        item.start()
    queries = jnp.dot(normalized, q_w[...], preferred_element_type=jnp.float32).astype(
        jnp.bfloat16
    )
    for item in kv_copies:
        item.wait_recv()
    keys = kv[:, :, 0:128].reshape(depth * rows, 128)
    values = kv[:, :, 128:256].reshape(depth * rows, 128)
    for head in range(heads):
        lanes = slice(head * 128, (head + 1) * 128)
        scores = lax.dot_general(
            queries[:, lanes],
            keys,
            (((1,), (1,)), ((), ())),
            preferred_element_type=jnp.float32,
        )
        scores = scores * (128**-0.5) + bias[head]
        weights = jnp.exp(scores - jnp.max(scores, axis=1, keepdims=True))
        denominator = jnp.sum(weights, axis=1, keepdims=True)
        summed = jnp.dot(weights.astype(jnp.bfloat16), values, preferred_element_type=jnp.float32)
        attended[:, lanes] = (summed / denominator).astype(jnp.bfloat16)
    mixed_ref[...] = jnp.dot(
        attended[...], out_w[...], preferred_element_type=jnp.float32
    ).astype(jnp.bfloat16)

    pl.when(z > 0)(to_left.wait_send)
    pl.when(z < depth - 1)(to_right.wait_send)
    for i in range(number):
        own_to_x(i).wait_send()
        own_to_core(i).wait_send()
        pass_on(i).wait_send()
        each_across(i, lambda item: item.wait_send())
        each_pass(i, lambda item: item.wait_send(), False)
    for item in code_copies + edge_copies + stat_copies + pool_copies + kv_copies:
        item.wait_send()


def fused_shards(
    signal,
    bases,
    base_table,
    conv_weight,
    batch_norm_gain,
    norm_bias,
    proj_weight,
    attn_gain,
    q_weight,
    k_weight,
    v_weight,
    bias_table,
    buckets,
    out_weight,
):
    positions, channels = signal.shape[1:]
    rows = positions // PLANES
    devices, depth = lax.axis_size("dp"), lax.axis_size("seq")
    width = conv_weight.shape[0]
    share = conv_weight.shape[2]
    heads, classes = bias_table.shape[:2]
    model = proj_weight.shape[1]
    taps = jnp.transpose(conv_weight, (0, 2, 1))
    cuts = tuple(
        slice(start, min(start + 256, channels)) for start in range(0, channels, 256)
    )
    number = len(cuts)
    vmem = pl.BlockSpec(memory_space=pltpu.VMEM)
    anywhere = pl.BlockSpec(memory_space=pl.ANY)
    dma = pltpu.SemaphoreType.DMA
    narrow, wide = jnp.bfloat16, jnp.float32
    tokens, mixed = pl.pallas_call(
        functools.partial(block_kernel, cuts),
        out_shape=[jax.ShapeDtypeStruct((rows, model), narrow)] * 2,
        in_specs=[
            anywhere,
            vmem,
            vmem,
            anywhere,
            vmem,
            vmem,
            anywhere,
            vmem,
            anywhere,
            anywhere,
            anywhere,
            vmem,
            vmem,
            anywhere,
        ],
        out_specs=[vmem, vmem],
        scratch_shapes=[
            pltpu.VMEM((positions, channels), narrow),
            pltpu.VMEM((channels // 128, positions, 128), wide),
            pltpu.VMEM((4, PLANES + width - 1, rows, channels), narrow),
            pltpu.VMEM((2, width, share, channels), narrow),
            pltpu.VMEM((4, 2, positions, share), wide),
            pltpu.VMEM((2, 2, 16, channels), narrow),
            pltpu.VMEM((4, 16, channels), narrow),
            pltpu.VMEM((depth, classes, rows), narrow),
            pltpu.VMEM((2 * depth, 2, 8, share), wide),
            pltpu.VMEM((4, 2, rows, share), narrow),
            pltpu.VMEM((devices, rows, share), narrow),
            pltpu.VMEM((depth, rows, 256), narrow),
            pltpu.VMEM((heads, rows, depth * rows), wide),
            pltpu.VMEM(proj_weight.shape, narrow),
            pltpu.VMEM(q_weight.shape, narrow),
            pltpu.VMEM((model, 256), narrow),
            pltpu.VMEM(out_weight.shape, narrow),
            pltpu.VMEM((rows, q_weight.shape[1]), narrow),
            dma((7,)),
            dma((2,)),
            dma((2,)),
            dma((4,)),
            dma((4,)),
            dma((depth,)),
            dma((depth,)),
            dma((number,)),
            dma((number,)),
            dma((number,)),
            dma((number,)),
            dma((number,)),
            dma((number,)),
            dma((number,)),
            dma((number,)),
            dma((number,)),
            dma((number,)),
            dma((2 * depth,)),
            dma((2 * depth,)),
            dma((4, 2)),
            dma((4, 2)),
            dma((depth,)),
            dma((depth,)),
        ],
        compiler_params=pltpu.CompilerParams(
            collective_id=0, has_side_effects=True, vmem_limit_bytes=52 * 1024 * 1024
        ),
        cost_estimate=pl.CostEstimate(
            flops=12_000_000_000, bytes_accessed=20_000_000, transcendentals=4_000_000
        ),
    )(
        signal[0],
        bases,
        base_table,
        taps,
        batch_norm_gain.reshape(devices, 1, share),
        norm_bias.reshape(devices, 1, share),
        proj_weight,
        attn_gain[None],
        q_weight,
        k_weight,
        v_weight,
        bias_table,
        buckets,
        out_weight,
    )
    return (tokens[None], mixed[None])


def solution(mesh):
    placed = (
        P("dp", "seq", None),
        P("dp", "seq"),
        P(),
        P(None, None, "dp"),
        P(),
        P(),
        P(),
        P(),
        P(),
        P(),
        P(),
        P(),
        P("dp", "seq"),
        P(),
    )
    whole_cube = mesh.shape["dp"] == 8 and mesh.shape["seq"] == 4
    return jax.shard_map(
        fused_shards if whole_cube else shards,
        mesh=mesh,
        in_specs=placed,
        out_specs=(P("dp", "seq", None), P("dp", "seq", None)),
        check_vma=False,
    )
```
